32 devices in a mesh: wall: 2 (over core), sx: 4 (over y, x), sy: 4 (over z).
Axes of the slice: x: 2, y: 2, z: 4, core: 2. Of those that a mesh axis runs over, the one named last changes fastest.
Arguments:
- forcing: float32 [4, 8, 8, 384], P('sx', 'sy', 'wall'), may hold values from -17 to 17
- pivot_inverse: float32 [4, 8, 8, 384, 384], P('sx', 'sy', 'wall'), may hold values from -1 to 5
- lower_face: float32 [4, 8, 8, 96, 96], P('sx', 'sy', 'wall'), may hold values from -1 to 2
- upper_face: float32 [4, 8, 8, 96, 96], P('sx', 'sy', 'wall'), may hold values from -1 to 2
- side_coupling: float32 [4, 8, 8, 4, 96, 96], P('sx', 'sy', 'wall'), may hold values from -0.3125 to 0.3125
- orientation: int32 [4, 8, 8, 4], P('sx', 'sy', 'wall'), may hold values from 0 to 3
Outputs:
- solution: float32 [4, 8, 8, 384], P('sx', 'sy', 'wall')
- relative_residual: float32 [], replicated
- forcing_rms: float32 [], replicated
The draws below stay inside these ranges and needn't reach their ends.
All inputs are finite; a program needn't handle non-finite values.
Results may differ from the reference program's by a relative error of at most 0.0003.
Values sent between devices are 32-bit elements; how exact they have to be, the bound alone decides.
A program may use at most 64 MiB of HBM per device.

```python
import math
import jax
import jax.numpy as jnp
from jax import lax

PTS = 4
VARS = 6
BLOCK = 384
FACE = 96
ITERS = 3
NLX = 4
NLY = 8
LINE_ELEMENTS = 8


def draw_forcing(key, part):
    full_shape = (NLX, NLY, LINE_ELEMENTS, BLOCK)
    position = lax.broadcasted_iota(jnp.int32, full_shape, 2).astype(jnp.float32) / (LINE_ELEMENTS - 1)
    values = jnp.clip(jax.random.normal(key, full_shape, jnp.float32), -4.0, 4.0)
    return values * jnp.exp(position * math.log(3.0))


def channel_rates(key, leading_dims):
    split_random_keys = jax.random.split(key, 3)
    lowest, highest = (0.5 / LINE_ELEMENTS, 0.15)
    falloff_factor = jnp.exp(jax.random.uniform(split_random_keys[0], (FACE,), jnp.float32, math.log(lowest), math.log(highest)))
    random_perturbation = jax.random.uniform(split_random_keys[1], leading_dims + (FACE,), jnp.float32, 0.7, 1.4)
    spike_threshold = jnp.where(jax.random.uniform(split_random_keys[2], leading_dims + (1,), jnp.float32) < 3.0 / LINE_ELEMENTS, 0.5, 1.0)
    return jnp.exp(-falloff_factor * random_perturbation) * spike_threshold


def draw_pivot_inverse(key, part):
    split_random_keys = jax.random.split(jax.random.fold_in(key, 11), 4)
    leading_dims = (NLX, NLY, LINE_ELEMENTS)
    full_shape = leading_dims + (BLOCK, BLOCK)
    scatter_part = jnp.clip(jax.random.normal(split_random_keys[0], full_shape, jnp.float32), -4.0, 4.0)
    middle = jnp.exp(jax.random.uniform(split_random_keys[1], leading_dims + (BLOCK,), jnp.float32, math.log(1.5), math.log(4.0)))
    upward = channel_rates(split_random_keys[2], leading_dims)
    downward = channel_rates(split_random_keys[3], leading_dims)
    row_ids = lax.broadcasted_iota(jnp.int32, (BLOCK, BLOCK), 0)
    col_ids = lax.broadcasted_iota(jnp.int32, (BLOCK, BLOCK), 1)
    offset = BLOCK - FACE
    upward_row = jnp.concatenate([jnp.zeros(leading_dims + (offset,), jnp.float32), upward], -1)
    downward_row = jnp.concatenate([downward, jnp.zeros(leading_dims + (offset,), jnp.float32)], -1)
    result = jnp.where(row_ids == col_ids, middle[..., :, None], scatter_part * (0.25 / math.sqrt(BLOCK)))
    result = result + jnp.where((row_ids >= offset) & (col_ids == row_ids - offset), upward_row[..., :, None], 0.0)
    result = result + jnp.where((row_ids < FACE) & (col_ids == row_ids + offset), downward_row[..., :, None], 0.0)
    return result


def face_coupling(key, salt):
    split_random_keys = jax.random.split(jax.random.fold_in(key, salt), 2)
    leading_dims = (NLX, NLY, LINE_ELEMENTS)
    full_shape = leading_dims + (FACE, FACE)
    scatter_part = jnp.clip(jax.random.normal(split_random_keys[0], full_shape, jnp.float32), -4.0, 4.0)
    gain_part = jax.random.uniform(split_random_keys[1], leading_dims + (FACE,), jnp.float32, 0.9, 1.0)
    row_ids = lax.broadcasted_iota(jnp.int32, (FACE, FACE), 0)
    col_ids = lax.broadcasted_iota(jnp.int32, (FACE, FACE), 1)
    return jnp.where(row_ids == col_ids, gain_part[..., :, None], 0.0) + scatter_part * (0.1 / math.sqrt(FACE))


def draw_lower_face(key, part):
    return face_coupling(key, 23)


def draw_upper_face(key, part):
    return face_coupling(key, 37)


def place_ends(values, stream_key, least, high):
    longest = values.shape.index(max(values.shape))
    spots = []
    for shift in (0, 1):
        where = [jax.random.randint(jax.random.fold_in(stream_key, axis), (), 0, length) for axis, length in enumerate(values.shape)]
        where[longest] = (where[longest] + shift) % values.shape[longest]
        spots.append(tuple(where))
    return values.at[spots[0]].set(least).at[spots[1]].set(high)


def shard_levels(own_key, shape, shards, low, largest):
    def one(dim, blocks):
        steps = jax.random.uniform(jax.random.fold_in(jax.random.fold_in(own_key, 6), dim), (blocks,), jnp.float32, low / len(shards), largest / len(shards))
        return jnp.repeat(jnp.exp(steps), shape[dim] // blocks).reshape((-1,) + (1,) * (len(shape) - dim - 1))

    gain = one(*shards[0])
    for cut in shards[1:]:
        gain = gain * one(*cut)
    return gain


def noise(key, shape, scale, bound, shards=(), held_as=jnp.bfloat16):
    values = scale * jax.random.normal(key, shape, jnp.float32)
    if shards:
        values = values * shard_levels(key, shape, shards, -0.22, 0.18)
    return jnp.clip(values, -bound, bound).astype(held_as)


def setup_inputs(seed: int = 0) -> dict:
    key_list = jax.random.split(jax.random.key(seed), 7)
    return {
        "forcing": draw_forcing(jax.random.fold_in(key_list[6], 71), 0),
        "pivot_inverse": draw_pivot_inverse(jax.random.fold_in(key_list[6], 71), 0),
        "lower_face": draw_lower_face(jax.random.fold_in(key_list[6], 71), 0),
        "upper_face": draw_upper_face(jax.random.fold_in(key_list[6], 71), 0),
        "side_coupling": noise(key_list[4], (NLX, NLY, LINE_ELEMENTS, 4, FACE, FACE), (4 * FACE) ** -0.5, 0.3125, ((0, 4), (1, 4), (2, 2)), jnp.float32),
        "orientation": place_ends(jax.random.randint(key_list[5], (NLX, NLY, LINE_ELEMENTS, 4), 0, 4), jax.random.fold_in(key_list[5], 1), 0, 3).astype(jnp.int32),
    }


precise = lax.Precision.HIGHEST

def face_traces(vector_in):
    leading = vector_in.shape[:-1]
    node_grid = vector_in.reshape(leading + (PTS, PTS, PTS, VARS))
    facets = [node_grid[..., :, :, 0, :], node_grid[..., :, :, PTS - 1, :], node_grid[..., :, 0, :, :], node_grid[..., :, PTS - 1, :, :]]
    flattened = [one_facet.reshape(leading + (FACE,)) for one_facet in facets]
    return jnp.stack(flattened, -2).reshape(leading + (4 * FACE,))

def lateral_term(vector_in, padded, side_coupling, orientation):
    single_row_block, rows_two = (vector_in.shape[0], vector_in.shape[1])
    beside_all = padded.reshape(padded.shape[:3] + (4, FACE))
    across = jnp.stack([beside_all[0:single_row_block, 1:rows_two + 1, :, 1], beside_all[2:single_row_block + 2, 1:rows_two + 1, :, 0], beside_all[1:single_row_block + 1, 0:rows_two, :, 3], beside_all[1:single_row_block + 1, 2:rows_two + 2, :, 2]], 3)
    shaped = across.reshape(across.shape[:4] + (PTS, PTS, VARS))
    turned = jnp.zeros(shaped.shape, jnp.float32)
    for quarter in range(4):
        picked = (orientation == quarter).astype(jnp.float32)[..., None, None, None]
        turned = turned + picked * jnp.rot90(shaped, quarter, axes=(4, 5))
    coupled = jnp.einsum('xyefab,xyefb->xyefa', side_coupling, turned.reshape(across.shape), precision=precise)
    pieces = coupled.reshape(across.shape[:4] + (PTS, PTS, VARS))
    result = jnp.zeros(vector_in.shape[:3] + (PTS, PTS, PTS, VARS), jnp.float32)
    result = result.at[:, :, :, :, :, 0, :].add(pieces[:, :, :, 0])
    result = result.at[:, :, :, :, :, PTS - 1, :].add(pieces[:, :, :, 1])
    result = result.at[:, :, :, :, 0, :, :].add(pieces[:, :, :, 2])
    result = result.at[:, :, :, :, PTS - 1, :, :].add(pieces[:, :, :, 3])
    return result.reshape(vector_in.shape)

def precondition(resid, pivot_inverse, lower_face, upper_face):
    elements = resid.shape[2]
    carried = jnp.zeros(resid.shape[:2] + (FACE,), jnp.float32)
    reduced = []
    for i in range(elements):
        lowered = jnp.einsum('xyab,xyb->xya', lower_face[:, :, i], carried, precision=precise)
        block_row = jnp.concatenate([resid[:, :, i, :FACE] - lowered, resid[:, :, i, FACE:]], -1)
        reduced.append(block_row)
        carried = jnp.einsum('xyab,xyb->xya', pivot_inverse[:, :, i, BLOCK - FACE:, :], block_row, precision=precise)
    carried = jnp.zeros(resid.shape[:2] + (FACE,), jnp.float32)
    solved = [None] * elements
    for i in reversed(range(elements)):
        raised = jnp.einsum('xyab,xyb->xya', upper_face[:, :, i], carried, precision=precise)
        block_row = jnp.concatenate([reduced[i][..., :BLOCK - FACE], reduced[i][..., BLOCK - FACE:] - raised], -1)
        answer = jnp.einsum('xyab,xyb->xya', pivot_inverse[:, :, i], block_row, precision=precise)
        solved[i] = answer
        carried = answer[..., :FACE]
    return jnp.stack(solved, 2)

def solve_small(matrix, vector):
    extent = matrix.shape[0]
    index_ids = jnp.arange(extent)
    for k in range(extent):
        factor_col = jnp.where(index_ids > k, matrix[:, k] / matrix[k, k], 0.0)
        matrix = matrix - factor_col[:, None] * matrix[k][None, :]
        vector = vector - factor_col * vector[k]
    solved = jnp.zeros((extent,), jnp.float32)
    for k in reversed(range(extent)):
        solved = solved.at[k].set((vector[k] - jnp.sum(matrix[k] * solved)) / matrix[k, k])
    return solved

def least_squares(hessenberg, initial_norm):
    target = jnp.zeros((hessenberg.shape[0],), jnp.float32).at[0].set(initial_norm)
    normal = jnp.dot(hessenberg.T, hessenberg, precision=precise)
    weights = solve_small(normal, jnp.dot(hessenberg.T, target, precision=precise))
    misfit = target - jnp.dot(hessenberg, weights, precision=precise)
    return (weights, jnp.sqrt(jnp.sum(misfit * misfit)) / initial_norm)

def reference(forcing, pivot_inverse, lower_face, upper_face, side_coupling, orientation):
    squares = jnp.sum(forcing * forcing)
    forcing_rms = jnp.sqrt(squares / (NLX * NLY * LINE_ELEMENTS * BLOCK))
    initial_norm = jnp.sqrt(squares)
    krylov = [forcing / initial_norm]
    directions = []
    columns = []
    for j in range(ITERS):
        direction = precondition(krylov[j], pivot_inverse, lower_face, upper_face)
        directions.append(direction)
        traces = face_traces(direction)
        padded = jnp.pad(traces, ((1, 1), (1, 1), (0, 0), (0, 0)))
        vector_w = krylov[j] + lateral_term(direction, padded, side_coupling, orientation)
        listed = []
        for i in range(j + 1):
            projected = jnp.sum(vector_w * krylov[i])
            vector_w = vector_w - projected * krylov[i]
            listed.append(projected)
        length = jnp.sqrt(jnp.sum(vector_w * vector_w))
        krylov.append(vector_w / length)
        columns.append(jnp.concatenate([jnp.stack(listed), length[None], jnp.zeros((ITERS - 1 - j,), jnp.float32)]))
    hessenberg = jnp.stack(columns, 1)
    weights, relative = least_squares(hessenberg, initial_norm)
    solution = weights[0] * directions[0]
    for j in range(1, ITERS):
        solution = solution + weights[j] * directions[j]
    return (solution, relative, forcing_rms)
```

```python
import functools

import jax
import jax.numpy as jnp
import numpy as np
from jax import lax
from jax.experimental import pallas as pl
from jax.experimental.pallas import tpu as pltpu
from jax.sharding import PartitionSpec as P

PTS = 4
VARS = 6
BLOCK = 384
FACE = 96
ITERS = 3
LANES = 128
TAIL = BLOCK - FACE
MESH = pl.DeviceIdType.MESH
PAIRS = [(a, b) for a in range(ITERS + 1) for b in range(a, ITERS + 1)]


def face_nodes():
    ids = np.arange(BLOCK).reshape(PTS, PTS, PTS, VARS)
    return [ids[:, :, 0], ids[:, :, PTS - 1], ids[:, 0], ids[:, PTS - 1]]


def gather_matrices():
    faces = face_nodes()
    out = np.zeros((4, BLOCK, 4 * LANES), np.float32)
    for f, touching in enumerate((1, 0, 3, 2)):
        for turn in range(4):
            source = np.rot90(faces[touching], turn, axes=(0, 1)).reshape(-1)
            out[f, source, turn * LANES + np.arange(FACE)] = 1.0
    return out


def scatter_matrix():
    out = np.zeros((4 * FACE, BLOCK), np.float32)
    for f, nodes in enumerate(face_nodes()):
        out[f * FACE + np.arange(FACE), nodes.reshape(-1)] = 1.0
    return out


def split_rows(x):
    high = x.astype(jnp.bfloat16).astype(jnp.float32)
    rest = x - high
    middle = rest.astype(jnp.bfloat16).astype(jnp.float32)
    low = rest - middle
    pad = jnp.zeros_like(x)
    return jnp.concatenate([high, middle, low, pad], 0).astype(jnp.bfloat16)


def select_dot(x, chosen):
    rows = x.shape[0]
    y = jnp.dot(split_rows(x), chosen, preferred_element_type=jnp.float32)
    return y[:rows] + y[rows : 2 * rows] + y[2 * rows : 3 * rows]


def kernel(
    dims,
    total_entries,
    f_hbm,
    piv_hbm,
    low_hbm,
    up_hbm,
    side_hbm,
    ori_hbm,
    gat_hbm,
    sca_hbm,
    sol_ref,
    rel_ref,
    rms_ref,
    f_v,
    piv,
    low,
    up,
    side,
    ori,
    gat,
    sca,
    turned,
    ubuf,
    dbuf,
    yrow,
    fwd_out,
    fwd_in,
    bwd_out,
    bwd_in,
    hx_low,
    hx_high,
    hy_low,
    hy_high,
    gram_a,
    gram_b,
    load_sem,
    piv_sem,
    wall_sem,
    halo_sem,
    a_send,
    a_recv,
    b_send,
    b_recv,
):
    W, SX, SY = dims
    X, Y, E = f_v.shape[:3]
    L = X * Y
    N = L * E
    lines = [(x, y) for x in range(X) for y in range(Y)]
    wall, sx, sy = lax.axis_index("wall"), lax.axis_index("sx"), lax.axis_index("sy")
    rank = wall * SX + sx
    n_a = W * SX

    loads = [
        pltpu.make_async_copy(src, dst, load_sem.at[i])
        for i, (src, dst) in enumerate(
            [
                (f_hbm, f_v),
                (low_hbm, low),
                (up_hbm, up),
                (gat_hbm, gat),
                (side_hbm, side),
                (ori_hbm, ori),
                (sca_hbm, sca),
            ]
        )
    ]
    piv_loads = [
        pltpu.make_async_copy(piv_hbm.at[x, y, k], piv.at[x, y, k], piv_sem.at[(x * Y + y) * E + k])
        for x, y in lines
        for k in range(E)
    ]
    loads[0].start()
    for c in piv_loads:
        c.start()
    for c in loads[1:]:
        c.start()

    for ref in (fwd_in, bwd_in, hx_low, hx_high, hy_low, hy_high, fwd_out, bwd_out):
        ref[...] = jnp.zeros(ref.shape, jnp.float32)

    barrier = pltpu.get_barrier_semaphore()

    def group_a(t):
        target = lax.rem(rank + t, n_a)
        return {"wall": target // SX, "sx": lax.rem(target, SX)}

    def group_b(t):
        return {"sy": lax.rem(sy + t, SY)}

    for t in range(1, n_a):
        pl.semaphore_signal(barrier, inc=1, device_id=group_a(t), device_id_type=MESH)
    for t in range(1, SY):
        pl.semaphore_signal(barrier, inc=1, device_id=group_b(t), device_id_type=MESH)

    loads[0].wait()
    ubuf[0] = jnp.concatenate([f_v[x, y] for x, y in lines], 0)
    lane = lax.broadcasted_iota(jnp.int32, (1, LANES), 1)

    corner_pad = jnp.zeros((LANES - FACE, LANES), jnp.float32)
    for e in range(N):
        x, y, k = e // E // Y, e // E % Y, e % E
        piv_loads[e].wait()
        turned[0, e] = jnp.concatenate([piv[x, y, k, TAIL:, :LANES], corner_pad], 0).T[:FACE]
        turned[1, e] = jnp.concatenate([piv[x, y, k, :FACE, :LANES], corner_pad], 0).T[:FACE]
        turned[2, e] = jnp.concatenate([piv[x, y, k, :FACE, TAIL - 32 :], corner_pad], 0).T[32:]
    for c in loads[1:]:
        c.wait()
    if n_a + SY > 2:
        pl.semaphore_wait(barrier, n_a + SY - 2)

    def put(columns, e, column):
        return jnp.where(lane == e, column, columns)

    def rows_of(columns):
        return columns.T[:N]

    def remote(src, dst, send, recv, device):
        return pltpu.make_async_remote_copy(
            src_ref=src, dst_ref=dst, send_sem=send, recv_sem=recv, device_id=device, device_id_type=MESH
        )

    def halo_copies(j):
        s = halo_sem
        return [
            (sx < SX - 1, sx > 0, remote(dbuf.at[j, X - 1], hx_low.at[j], s.at[0, 0, j], s.at[1, 0, j], {"sx": lax.rem(sx + 1, SX)})),
            (sx > 0, sx < SX - 1, remote(dbuf.at[j, 0], hx_high.at[j], s.at[0, 1, j], s.at[1, 1, j], {"sx": lax.rem(sx + SX - 1, SX)})),
            (sy < SY - 1, sy > 0, remote(dbuf.at[j, :, Y - 1], hy_low.at[j], s.at[0, 2, j], s.at[1, 2, j], {"sy": lax.rem(sy + 1, SY)})),
            (sy > 0, sy < SY - 1, remote(dbuf.at[j, :, 0], hy_high.at[j], s.at[0, 3, j], s.at[1, 3, j], {"sy": lax.rem(sy + SY - 1, SY)})),
        ]

    def wall_copies(j):
        s = wall_sem
        return (
            remote(fwd_out.at[j], fwd_in.at[j], s.at[0, 0, j], s.at[1, 0, j], {"wall": lax.rem(wall + 1, W)}),
            remote(bwd_out.at[j], bwd_in.at[j], s.at[0, 1, j], s.at[1, 1, j], {"wall": lax.rem(wall + W - 1, W)}),
        )

    def step(j, carry):
        columns = jnp.zeros((BLOCK, LANES), jnp.float32)
        for e in range(N):
            x, y, k = e // E // Y, e // E % Y, e % E
            r = ubuf[j, e : e + 1, :]
            part = piv[x, y, k, :, :LANES] * r[:, :LANES]
            for c in range(1, BLOCK // LANES):
                part += piv[x, y, k, :, c * LANES : (c + 1) * LANES] * r[:, c * LANES : (c + 1) * LANES]
            columns = put(columns, e, jnp.sum(part, 1, keepdims=True))
        y_all = rows_of(columns)
        yrow[...] = y_all
        ahead = y_all[:, TAIL:]

        forward, backward = wall_copies(j)

        @pl.when(wall > 0)
        def _():
            forward.wait_recv()

        u_cols = [None] * N
        for l, (x, y) in enumerate(lines):
            s = fwd_in[j, l : l + 1, :FACE]
            for k in range(E):
                e = l * E + k
                u_cols[e] = jnp.sum(low[x, y, k] * s, 1, keepdims=True)
                s = ahead[e : e + 1] - jnp.sum(turned[0, e, :, :FACE] * u_cols[e], 0, keepdims=True)
            fwd_out[j, l : l + 1, :FACE] = s

        @pl.when(wall < W - 1)
        def _():
            forward.start()

        trailing = []
        u_columns = jnp.zeros((FACE, LANES), jnp.float32)
        for e in range(N):
            trailing.append(
                yrow[e : e + 1, :FACE] - jnp.sum(turned[1, e, :, :FACE] * u_cols[e], 0, keepdims=True)
            )
            u_columns = put(u_columns, e, u_cols[e])
        u_rows = rows_of(jnp.concatenate([u_columns, corner_pad], 0))

        @pl.when(wall < W - 1)
        def _():
            backward.wait_recv()

        v_columns = jnp.zeros((FACE, LANES), jnp.float32)
        for l, (x, y) in enumerate(lines):
            t = bwd_in[j, l : l + 1, :FACE]
            for k in reversed(range(E)):
                e = l * E + k
                v = jnp.sum(up[x, y, k] * t, 1, keepdims=True)
                v_columns = put(v_columns, e, v)
                t = trailing[e] - jnp.sum(turned[2, e, :, :FACE] * v, 0, keepdims=True)
            bwd_out[j, l : l + 1, :FACE] = t

        @pl.when(wall > 0)
        def _():
            backward.start()

        v_rows = rows_of(jnp.concatenate([corner_pad, v_columns], 0))
        columns = jnp.zeros((BLOCK, LANES), jnp.float32)
        for e in range(N):
            x, y, k = e // E // Y, e // E % Y, e % E
            part = piv[x, y, k, :, :LANES] * u_rows[e : e + 1]
            part += piv[x, y, k, :, BLOCK - LANES :] * v_rows[e : e + 1]
            columns = put(columns, e, jnp.sum(part, 1, keepdims=True))
        d = yrow[...] - rows_of(columns)
        for l, (x, y) in enumerate(lines):
            dbuf[j, x, y] = d[l * E : (l + 1) * E]

        halos = halo_copies(j)
        for sends, _, copy in halos:
            pl.when(sends)(copy.start)
        for _, receives, copy in halos:
            pl.when(receives)(copy.wait_recv)

        beside = [[], [], [], []]
        for x, y in lines:
            beside[0].append(dbuf[j, x - 1, y] if x > 0 else hx_low[j, y])
            beside[1].append(dbuf[j, x + 1, y] if x < X - 1 else hx_high[j, y])
            beside[2].append(dbuf[j, x, y - 1] if y > 0 else hy_low[j, x])
            beside[3].append(dbuf[j, x, y + 1] if y < Y - 1 else hy_high[j, x])
        turns = jnp.concatenate([ori[x, y] for x, y in lines], 0)
        blocks = []
        for f in range(4):
            all_turns = select_dot(jnp.concatenate(beside[f], 0), gat[f])
            across = all_turns[:, :LANES]
            for q in range(1, 4):
                across = jnp.where(turns[:, f : f + 1] == q, all_turns[:, q * LANES : (q + 1) * LANES], across)
            across = across[:, :FACE]
            block = jnp.zeros((FACE, LANES), jnp.float32)
            for e in range(N):
                x, y, k = e // E // Y, e // E % Y, e % E
                block = put(block, e, jnp.sum(side[x, y, k, f] * across[e : e + 1], 1, keepdims=True))
            blocks.append(block)
        coupled = rows_of(jnp.concatenate(blocks, 0))
        ubuf[j + 1] = select_dot(coupled, sca[...])
        return carry

    lax.fori_loop(0, ITERS, step, 0)

    sums = []
    for a, b in PAIRS:
        product = ubuf[a] * ubuf[b]
        folded = product[:, :LANES]
        for c in range(1, BLOCK // LANES):
            folded += product[:, c * LANES : (c + 1) * LANES]
        sums.append(jnp.sum(folded, 0, keepdims=True))
    sums.append(jnp.zeros((16 - len(PAIRS), LANES), jnp.float32))
    gram_a[rank] = jnp.concatenate(sums, 0)
    a_copies = [
        remote(gram_a.at[rank], gram_a.at[rank], a_send.at[t - 1], a_recv.at[t - 1], group_a(t)) for t in range(1, n_a)
    ]
    for c in a_copies:
        c.start()
    for t in range(1, n_a):
        source = lax.rem(rank + n_a - t, n_a)
        remote(gram_a.at[source], gram_a.at[source], a_send.at[t - 1], a_recv.at[t - 1], group_a(t)).wait_recv()
    gram = gram_a[0]
    for i in range(1, n_a):
        gram += gram_a[i]
    gram_b[sy] = gram
    b_copies = [
        remote(gram_b.at[sy], gram_b.at[sy], b_send.at[t - 1], b_recv.at[t - 1], group_b(t)) for t in range(1, SY)
    ]
    for c in b_copies:
        c.start()
    for t in range(1, SY):
        source = lax.rem(sy + SY - t, SY)
        remote(gram_b.at[source], gram_b.at[source], b_send.at[t - 1], b_recv.at[t - 1], group_b(t)).wait_recv()
    gram = gram_b[0]
    for i in range(1, SY):
        gram += gram_b[i]
    gram = jnp.sum(gram, 1, keepdims=True)
    g = {}
    for i, (a, b) in enumerate(PAIRS):
        g[a, b] = gram[i : i + 1]

    M = ITERS
    zero = jnp.zeros((1, 1), jnp.float32)
    tri = [[zero] * (M + 1) for _ in range(M + 1)]
    for i in range(M + 1):
        rest = g[i, i]
        for p in range(i):
            rest = rest - tri[p][i] * tri[p][i]
        tri[i][i] = jnp.sqrt(jnp.maximum(rest, 0.0))
        for c in range(i + 1, M + 1):
            rest = g[i, c]
            for p in range(i):
                rest = rest - tri[p][i] * tri[p][c]
            tri[i][c] = rest / tri[i][i]
    hess = [[zero] * M for _ in range(M + 1)]
    for i in range(M + 1):
        for c in range(M):
            value = tri[i][c + 1]
            for p in range(c):
                value = value - hess[i][p] * tri[p][c]
            hess[i][c] = value / tri[c][c]
    for c in range(M):
        hess[c][c] = hess[c][c] + 1.0
    for c in range(M):
        for i in range(c + 2, M + 1):
            hess[i][c] = zero
    start = tri[0][0]
    normal = [[zero] * M for _ in range(M)]
    for a in range(M):
        for b in range(a, M):
            value = hess[0][a] * hess[0][b]
            for i in range(1, M + 1):
                value = value + hess[i][a] * hess[i][b]
            normal[a][b] = normal[b][a] = value
    right = [hess[0][a] * start for a in range(M)]
    for k in range(M):
        for i in range(k + 1, M):
            factor = normal[i][k] / normal[k][k]
            for c in range(k, M):
                normal[i][c] = normal[i][c] - factor * normal[k][c]
            right[i] = right[i] - factor * right[k]
    weights = [zero] * M
    for k in reversed(range(M)):
        value = right[k]
        for c in range(k + 1, M):
            value = value - normal[k][c] * weights[c]
        weights[k] = value / normal[k][k]
    squared = zero
    for i in range(M + 1):
        miss = start if i == 0 else zero
        for c in range(M):
            miss = miss - hess[i][c] * weights[c]
        squared = squared + miss * miss
    rel_ref[0] = (jnp.sqrt(squared) / start)[0, 0]
    rms_ref[0] = jnp.sqrt(g[0, 0] / total_entries)[0, 0]
    mixed = [zero] * M
    for k in reversed(range(M)):
        value = weights[k]
        for c in range(k + 1, M):
            value = value - tri[k][c] * mixed[c]
        mixed[k] = value / tri[k][k]
    for x, y in lines:
        out = mixed[0] * dbuf[0, x, y]
        for k in range(1, M):
            out = out + mixed[k] * dbuf[k, x, y]
        sol_ref[x, y] = out

    for c in a_copies + b_copies:
        c.wait_send()
    for j in range(ITERS):
        forward, backward = wall_copies(j)
        pl.when(wall < W - 1)(forward.wait_send)
        pl.when(wall > 0)(backward.wait_send)
        for sends, _, copy in halo_copies(j):
            pl.when(sends)(copy.wait_send)


def shards(dims, forcing, pivot_inverse, lower_face, upper_face, side_coupling, orientation):
    W, SX, SY = dims
    X, Y, E = forcing.shape[:3]
    L, N = X * Y, X * Y * E
    total_entries = forcing.size * W * SX * SY
    gather = jnp.asarray(gather_matrices(), jnp.bfloat16)
    scatter = jnp.asarray(scatter_matrix(), jnp.bfloat16)
    operands = (forcing, pivot_inverse, lower_face, upper_face, side_coupling, orientation, gather, scatter)
    f32 = jnp.float32
    dma = pltpu.SemaphoreType.DMA
    solution_out, relative, rms = pl.pallas_call(
        functools.partial(kernel, dims, total_entries),
        out_shape=(
            jax.ShapeDtypeStruct(forcing.shape, f32),
            jax.ShapeDtypeStruct((1,), f32),
            jax.ShapeDtypeStruct((1,), f32),
        ),
        in_specs=[pl.BlockSpec(memory_space=pl.ANY)] * len(operands),
        out_specs=(
            pl.BlockSpec(memory_space=pltpu.VMEM),
            pl.BlockSpec(memory_space=pltpu.SMEM),
            pl.BlockSpec(memory_space=pltpu.SMEM),
        ),
        scratch_shapes=[pltpu.VMEM(a.shape, a.dtype) for a in operands]
        + [
            pltpu.VMEM((3, N, FACE, LANES), f32),
            pltpu.VMEM((ITERS + 1, N, BLOCK), f32),
            pltpu.VMEM((ITERS, X, Y, E, BLOCK), f32),
            pltpu.VMEM((N, BLOCK), f32),
            pltpu.VMEM((ITERS, L, LANES), f32),
            pltpu.VMEM((ITERS, L, LANES), f32),
            pltpu.VMEM((ITERS, L, LANES), f32),
            pltpu.VMEM((ITERS, L, LANES), f32),
            pltpu.VMEM((ITERS, Y, E, BLOCK), f32),
            pltpu.VMEM((ITERS, Y, E, BLOCK), f32),
            pltpu.VMEM((ITERS, X, E, BLOCK), f32),
            pltpu.VMEM((ITERS, X, E, BLOCK), f32),
            pltpu.VMEM((W * SX, 16, LANES), f32),
            pltpu.VMEM((SY, 16, LANES), f32),
            dma((7,)),
            dma((N,)),
            dma((2, 2, ITERS)),
            dma((2, 4, ITERS)),
            dma((max(W * SX - 1, 1),)),
            dma((max(W * SX - 1, 1),)),
            dma((max(SY - 1, 1),)),
            dma((max(SY - 1, 1),)),
        ],
        compiler_params=pltpu.CompilerParams(
            collective_id=0, has_side_effects=True, vmem_limit_bytes=40 * 1024 * 1024
        ),
    )(*operands)
    return solution_out, relative.reshape(()), rms.reshape(())


def solution(mesh):
    dims = (mesh.shape["wall"], mesh.shape["sx"], mesh.shape["sy"])
    return jax.shard_map(
        functools.partial(shards, dims),
        mesh=mesh,
        in_specs=(
            P("sx", "sy", "wall", None),
            P("sx", "sy", "wall", None, None),
            P("sx", "sy", "wall", None, None),
            P("sx", "sy", "wall", None, None),
            P("sx", "sy", "wall", None, None, None),
            P("sx", "sy", "wall", None),
        ),
        out_specs=(P("sx", "sy", "wall", None), P(), P()),
        check_vma=False,
    )
```

```python
import functools

import jax
import jax.numpy as jnp
import numpy as np
from jax import lax
from jax.experimental import pallas as pl
from jax.experimental.pallas import tpu as pltpu
from jax.sharding import PartitionSpec as P

PTS = 4
VARS = 6
BLOCK = 384
FACE = 96
ITERS = 3
LANES = 128
TAIL = BLOCK - FACE
MESH = pl.DeviceIdType.MESH
PAIRS = [(a, b) for a in range(ITERS + 1) for b in range(a, ITERS + 1)]


def face_nodes():
    ids = np.arange(BLOCK).reshape(PTS, PTS, PTS, VARS)
    return [ids[:, :, 0], ids[:, :, PTS - 1], ids[:, 0], ids[:, PTS - 1]]


def gather_matrices():
    faces = face_nodes()
    out = np.zeros((4, BLOCK, 4 * LANES), np.float32)
    for f, touching in enumerate((1, 0, 3, 2)):
        for turn in range(4):
            source = np.rot90(faces[touching], turn, axes=(0, 1)).reshape(-1)
            out[f, source, turn * LANES + np.arange(FACE)] = 1.0
    return out


def scatter_matrix():
    out = np.zeros((4 * FACE, BLOCK), np.float32)
    for f, nodes in enumerate(face_nodes()):
        out[f * FACE + np.arange(FACE), nodes.reshape(-1)] = 1.0
    return out


def split_rows(x):
    high = x.astype(jnp.bfloat16).astype(jnp.float32)
    rest = x - high
    middle = rest.astype(jnp.bfloat16).astype(jnp.float32)
    low = rest - middle
    pad = jnp.zeros_like(x)
    return jnp.concatenate([high, middle, low, pad], 0).astype(jnp.bfloat16)


def select_dot(x, chosen):
    rows = x.shape[0]
    y = jnp.dot(split_rows(x), chosen, preferred_element_type=jnp.float32)
    return y[:rows] + y[rows : 2 * rows] + y[2 * rows : 3 * rows]


def lane_sums(part):
    high = part.astype(jnp.bfloat16)
    low = (part - high.astype(jnp.float32)).astype(jnp.bfloat16)
    ones = jnp.ones((16, part.shape[1]), jnp.bfloat16)
    if part.shape[1] == LANES:
        high, low = jnp.concatenate([high, low], 1), None
        ones = jnp.ones((16, 2 * LANES), jnp.bfloat16)

    def total(rows):
        return lax.dot_general(ones, rows, (((1,), (1,)), ((), ())), preferred_element_type=jnp.float32)

    sums = total(high)
    return (sums if low is None else sums + total(low))[:1]


def kernel(
    dims,
    total_entries,
    f_hbm,
    piv_hbm,
    low_hbm,
    up_hbm,
    side_hbm,
    ori_hbm,
    gat_hbm,
    sca_hbm,
    sol_ref,
    rel_ref,
    rms_ref,
    f_v,
    piv,
    low,
    up,
    side,
    ori,
    gat,
    sca,
    turned,
    ubuf,
    dbuf,
    yrow,
    fwd_out,
    fwd_in,
    bwd_out,
    bwd_in,
    hx_low,
    hx_high,
    hy_low,
    hy_high,
    gram_a,
    gram_b,
    load_sem,
    piv_sem,
    wall_sem,
    halo_sem,
    a_send,
    a_recv,
    b_send,
    b_recv,
):
    W, SX, SY = dims
    X, Y, E = f_v.shape[:3]
    L = X * Y
    N = L * E
    lines = [(x, y) for x in range(X) for y in range(Y)]
    wall, sx, sy = lax.axis_index("wall"), lax.axis_index("sx"), lax.axis_index("sy")
    rank = wall * SX + sx
    n_a = W * SX

    loads = [
        pltpu.make_async_copy(src, dst, load_sem.at[i])
        for i, (src, dst) in enumerate(
            [
                (f_hbm, f_v),
                (low_hbm, low),
                (up_hbm, up),
                (gat_hbm, gat),
                (side_hbm, side),
                (ori_hbm, ori),
                (sca_hbm, sca),
            ]
        )
    ]
    piv_loads = [
        pltpu.make_async_copy(piv_hbm.at[x, y, k], piv.at[x, y, k], piv_sem.at[(x * Y + y) * E + k])
        for x, y in lines
        for k in range(E)
    ]
    loads[0].start()
    for c in piv_loads:
        c.start()
    for c in loads[1:]:
        c.start()

    for ref in (fwd_in, bwd_in, hx_low, hx_high, hy_low, hy_high, fwd_out, bwd_out):
        ref[...] = jnp.zeros(ref.shape, jnp.float32)

    barrier = pltpu.get_barrier_semaphore()

    def group_a(t):
        target = lax.rem(rank + t, n_a)
        return {"wall": target // SX, "sx": lax.rem(target, SX)}

    def group_b(t):
        return {"sy": lax.rem(sy + t, SY)}

    for t in range(1, n_a):
        pl.semaphore_signal(barrier, inc=1, device_id=group_a(t), device_id_type=MESH)
    for t in range(1, SY):
        pl.semaphore_signal(barrier, inc=1, device_id=group_b(t), device_id_type=MESH)

    loads[0].wait()
    ubuf[0] = jnp.concatenate([f_v[x, y] for x, y in lines], 0)
    lane = lax.broadcasted_iota(jnp.int32, (1, LANES), 1)

    corner_pad = jnp.zeros((LANES - FACE, LANES), jnp.float32)
    for e in range(N):
        x, y, k = e // E // Y, e // E % Y, e % E
        piv_loads[e].wait()
        turned[0, e] = jnp.concatenate([piv[x, y, k, TAIL:, :LANES], corner_pad], 0).T[:FACE]
        turned[1, e] = jnp.concatenate([piv[x, y, k, :FACE, :LANES], corner_pad], 0).T[:FACE]
        turned[2, e] = jnp.concatenate([piv[x, y, k, :FACE, TAIL - 32 :], corner_pad], 0).T[32:]
    for c in loads[1:]:
        c.wait()
    if n_a + SY > 2:
        pl.semaphore_wait(barrier, n_a + SY - 2)

    def put(columns, e, column):
        return jnp.where(lane == e, column, columns)

    row_ids = lax.broadcasted_iota(jnp.int32, (N, 1), 0)

    def put_row(rows, e, row):
        return jnp.where(row_ids == e, row, rows)

    def rows_of(columns):
        return columns.T[:N]

    def remote(src, dst, send, recv, device):
        return pltpu.make_async_remote_copy(
            src_ref=src, dst_ref=dst, send_sem=send, recv_sem=recv, device_id=device, device_id_type=MESH
        )

    def halo_copies(j):
        s = halo_sem
        return [
            (sx < SX - 1, sx > 0, remote(dbuf.at[j, X - 1], hx_low.at[j], s.at[0, 0, j], s.at[1, 0, j], {"sx": lax.rem(sx + 1, SX)})),
            (sx > 0, sx < SX - 1, remote(dbuf.at[j, 0], hx_high.at[j], s.at[0, 1, j], s.at[1, 1, j], {"sx": lax.rem(sx + SX - 1, SX)})),
            (sy < SY - 1, sy > 0, remote(dbuf.at[j, :, Y - 1], hy_low.at[j], s.at[0, 2, j], s.at[1, 2, j], {"sy": lax.rem(sy + 1, SY)})),
            (sy > 0, sy < SY - 1, remote(dbuf.at[j, :, 0], hy_high.at[j], s.at[0, 3, j], s.at[1, 3, j], {"sy": lax.rem(sy + SY - 1, SY)})),
        ]

    def wall_copies(j):
        s = wall_sem
        return (
            remote(fwd_out.at[j], fwd_in.at[j], s.at[0, 0, j], s.at[1, 0, j], {"wall": lax.rem(wall + 1, W)}),
            remote(bwd_out.at[j], bwd_in.at[j], s.at[0, 1, j], s.at[1, 1, j], {"wall": lax.rem(wall + W - 1, W)}),
        )

    def step(j, carry):
        y_all = jnp.zeros((N, BLOCK), jnp.float32)
        for e in range(N):
            x, y, k = e // E // Y, e // E % Y, e % E
            r = ubuf[j, e : e + 1, :]
            part = piv[x, y, k, :, :LANES] * r[:, :LANES]
            for c in range(1, BLOCK // LANES):
                part += piv[x, y, k, :, c * LANES : (c + 1) * LANES] * r[:, c * LANES : (c + 1) * LANES]
            y_all = put_row(y_all, e, lane_sums(part))
        yrow[...] = y_all
        ahead = y_all[:, TAIL:]

        forward, backward = wall_copies(j)

        @pl.when(wall > 0)
        def _():
            forward.wait_recv()

        u_cols = [None] * N
        for l, (x, y) in enumerate(lines):
            s = fwd_in[j, l : l + 1, :FACE]
            for k in range(E):
                e = l * E + k
                u_cols[e] = jnp.sum(low[x, y, k] * s, 1, keepdims=True)
                s = ahead[e : e + 1] - jnp.sum(turned[0, e, :, :FACE] * u_cols[e], 0, keepdims=True)
            fwd_out[j, l : l + 1, :FACE] = s

        @pl.when(wall < W - 1)
        def _():
            forward.start()

        trailing = []
        u_columns = jnp.zeros((FACE, LANES), jnp.float32)
        for e in range(N):
            trailing.append(
                yrow[e : e + 1, :FACE] - jnp.sum(turned[1, e, :, :FACE] * u_cols[e], 0, keepdims=True)
            )
            u_columns = put(u_columns, e, u_cols[e])
        u_rows = rows_of(jnp.concatenate([u_columns, corner_pad], 0))

        @pl.when(wall < W - 1)
        def _():
            backward.wait_recv()

        v_columns = jnp.zeros((FACE, LANES), jnp.float32)
        for l, (x, y) in enumerate(lines):
            t = bwd_in[j, l : l + 1, :FACE]
            for k in reversed(range(E)):
                e = l * E + k
                v = jnp.sum(up[x, y, k] * t, 1, keepdims=True)
                v_columns = put(v_columns, e, v)
                t = trailing[e] - jnp.sum(turned[2, e, :, :FACE] * v, 0, keepdims=True)
            bwd_out[j, l : l + 1, :FACE] = t

        @pl.when(wall > 0)
        def _():
            backward.start()

        v_rows = rows_of(jnp.concatenate([corner_pad, v_columns], 0))
        change = jnp.zeros((N, BLOCK), jnp.float32)
        for e in range(N):
            x, y, k = e // E // Y, e // E % Y, e % E
            part = piv[x, y, k, :, :LANES] * u_rows[e : e + 1]
            part += piv[x, y, k, :, BLOCK - LANES :] * v_rows[e : e + 1]
            change = put_row(change, e, lane_sums(part))
        d = yrow[...] - change
        for l, (x, y) in enumerate(lines):
            dbuf[j, x, y] = d[l * E : (l + 1) * E]

        halos = halo_copies(j)
        for sends, _, copy in halos:
            pl.when(sends)(copy.start)
        for _, receives, copy in halos:
            pl.when(receives)(copy.wait_recv)

        beside = [[], [], [], []]
        for x, y in lines:
            beside[0].append(dbuf[j, x - 1, y] if x > 0 else hx_low[j, y])
            beside[1].append(dbuf[j, x + 1, y] if x < X - 1 else hx_high[j, y])
            beside[2].append(dbuf[j, x, y - 1] if y > 0 else hy_low[j, x])
            beside[3].append(dbuf[j, x, y + 1] if y < Y - 1 else hy_high[j, x])
        turns = jnp.concatenate([ori[x, y] for x, y in lines], 0)
        picked = []
        for f in range(4):
            all_turns = select_dot(jnp.concatenate(beside[f], 0), gat[f])
            across = all_turns[:, :LANES]
            for q in range(1, 4):
                across = jnp.where(turns[:, f : f + 1] == q, all_turns[:, q * LANES : (q + 1) * LANES], across)
            picked.append(across[:, :FACE])
        coupled = jnp.zeros((N, 4 * FACE), jnp.float32)
        for e in range(N):
            x, y, k = e // E // Y, e // E % Y, e % E
            part = jnp.concatenate([side[x, y, k, f] * picked[f][e : e + 1] for f in range(4)], 0)
            coupled = put_row(coupled, e, lane_sums(part))
        ubuf[j + 1] = select_dot(coupled, sca[...])
        return carry

    lax.fori_loop(0, ITERS, step, 0)

    sums = []
    for a, b in PAIRS:
        product = ubuf[a] * ubuf[b]
        folded = product[:, :LANES]
        for c in range(1, BLOCK // LANES):
            folded += product[:, c * LANES : (c + 1) * LANES]
        sums.append(jnp.sum(folded, 0, keepdims=True))
    sums.append(jnp.zeros((16 - len(PAIRS), LANES), jnp.float32))
    gram_a[rank] = jnp.concatenate(sums, 0)
    a_copies = [
        remote(gram_a.at[rank], gram_a.at[rank], a_send.at[t - 1], a_recv.at[t - 1], group_a(t)) for t in range(1, n_a)
    ]
    for c in a_copies:
        c.start()
    for t in range(1, n_a):
        source = lax.rem(rank + n_a - t, n_a)
        remote(gram_a.at[source], gram_a.at[source], a_send.at[t - 1], a_recv.at[t - 1], group_a(t)).wait_recv()
    gram = gram_a[0]
    for i in range(1, n_a):
        gram += gram_a[i]
    gram_b[sy] = gram
    b_copies = [
        remote(gram_b.at[sy], gram_b.at[sy], b_send.at[t - 1], b_recv.at[t - 1], group_b(t)) for t in range(1, SY)
    ]
    for c in b_copies:
        c.start()
    for t in range(1, SY):
        source = lax.rem(sy + SY - t, SY)
        remote(gram_b.at[source], gram_b.at[source], b_send.at[t - 1], b_recv.at[t - 1], group_b(t)).wait_recv()
    gram = gram_b[0]
    for i in range(1, SY):
        gram += gram_b[i]
    gram = jnp.sum(gram, 1, keepdims=True)
    g = {}
    for i, (a, b) in enumerate(PAIRS):
        g[a, b] = gram[i : i + 1]

    M = ITERS
    zero = jnp.zeros((1, 1), jnp.float32)
    tri = [[zero] * (M + 1) for _ in range(M + 1)]
    for i in range(M + 1):
        rest = g[i, i]
        for p in range(i):
            rest = rest - tri[p][i] * tri[p][i]
        tri[i][i] = jnp.sqrt(jnp.maximum(rest, 0.0))
        for c in range(i + 1, M + 1):
            rest = g[i, c]
            for p in range(i):
                rest = rest - tri[p][i] * tri[p][c]
            tri[i][c] = rest / tri[i][i]
    hess = [[zero] * M for _ in range(M + 1)]
    for i in range(M + 1):
        for c in range(M):
            value = tri[i][c + 1]
            for p in range(c):
                value = value - hess[i][p] * tri[p][c]
            hess[i][c] = value / tri[c][c]
    for c in range(M):
        hess[c][c] = hess[c][c] + 1.0
    for c in range(M):
        for i in range(c + 2, M + 1):
            hess[i][c] = zero
    start = tri[0][0]
    normal = [[zero] * M for _ in range(M)]
    for a in range(M):
        for b in range(a, M):
            value = hess[0][a] * hess[0][b]
            for i in range(1, M + 1):
                value = value + hess[i][a] * hess[i][b]
            normal[a][b] = normal[b][a] = value
    right = [hess[0][a] * start for a in range(M)]
    for k in range(M):
        for i in range(k + 1, M):
            factor = normal[i][k] / normal[k][k]
            for c in range(k, M):
                normal[i][c] = normal[i][c] - factor * normal[k][c]
            right[i] = right[i] - factor * right[k]
    weights = [zero] * M
    for k in reversed(range(M)):
        value = right[k]
        for c in range(k + 1, M):
            value = value - normal[k][c] * weights[c]
        weights[k] = value / normal[k][k]
    squared = zero
    for i in range(M + 1):
        miss = start if i == 0 else zero
        for c in range(M):
            miss = miss - hess[i][c] * weights[c]
        squared = squared + miss * miss
    rel_ref[0] = (jnp.sqrt(squared) / start)[0, 0]
    rms_ref[0] = jnp.sqrt(g[0, 0] / total_entries)[0, 0]
    mixed = [zero] * M
    for k in reversed(range(M)):
        value = weights[k]
        for c in range(k + 1, M):
            value = value - tri[k][c] * mixed[c]
        mixed[k] = value / tri[k][k]
    for x, y in lines:
        out = mixed[0] * dbuf[0, x, y]
        for k in range(1, M):
            out = out + mixed[k] * dbuf[k, x, y]
        sol_ref[x, y] = out

    for c in a_copies + b_copies:
        c.wait_send()
    for j in range(ITERS):
        forward, backward = wall_copies(j)
        pl.when(wall < W - 1)(forward.wait_send)
        pl.when(wall > 0)(backward.wait_send)
        for sends, _, copy in halo_copies(j):
            pl.when(sends)(copy.wait_send)


def shards(dims, forcing, pivot_inverse, lower_face, upper_face, side_coupling, orientation):
    W, SX, SY = dims
    X, Y, E = forcing.shape[:3]
    L, N = X * Y, X * Y * E
    total_entries = forcing.size * W * SX * SY
    gather = jnp.asarray(gather_matrices(), jnp.bfloat16)
    scatter = jnp.asarray(scatter_matrix(), jnp.bfloat16)
    operands = (forcing, pivot_inverse, lower_face, upper_face, side_coupling, orientation, gather, scatter)
    f32 = jnp.float32
    dma = pltpu.SemaphoreType.DMA
    solution_out, relative, rms = pl.pallas_call(
        functools.partial(kernel, dims, total_entries),
        out_shape=(
            jax.ShapeDtypeStruct(forcing.shape, f32),
            jax.ShapeDtypeStruct((1,), f32),
            jax.ShapeDtypeStruct((1,), f32),
        ),
        in_specs=[pl.BlockSpec(memory_space=pltpu.HBM)] * len(operands),
        out_specs=(
            pl.BlockSpec(memory_space=pltpu.VMEM),
            pl.BlockSpec(memory_space=pltpu.SMEM),
            pl.BlockSpec(memory_space=pltpu.SMEM),
        ),
        scratch_shapes=[pltpu.VMEM(a.shape, a.dtype) for a in operands]
        + [
            pltpu.VMEM((3, N, FACE, LANES), f32),
            pltpu.VMEM((ITERS + 1, N, BLOCK), f32),
            pltpu.VMEM((ITERS, X, Y, E, BLOCK), f32),
            pltpu.VMEM((N, BLOCK), f32),
            pltpu.VMEM((ITERS, L, LANES), f32),
            pltpu.VMEM((ITERS, L, LANES), f32),
            pltpu.VMEM((ITERS, L, LANES), f32),
            pltpu.VMEM((ITERS, L, LANES), f32),
            pltpu.VMEM((ITERS, Y, E, BLOCK), f32),
            pltpu.VMEM((ITERS, Y, E, BLOCK), f32),
            pltpu.VMEM((ITERS, X, E, BLOCK), f32),
            pltpu.VMEM((ITERS, X, E, BLOCK), f32),
            pltpu.VMEM((W * SX, 16, LANES), f32),
            pltpu.VMEM((SY, 16, LANES), f32),
            dma((7,)),
            dma((N,)),
            dma((2, 2, ITERS)),
            dma((2, 4, ITERS)),
            dma((max(W * SX - 1, 1),)),
            dma((max(W * SX - 1, 1),)),
            dma((max(SY - 1, 1),)),
            dma((max(SY - 1, 1),)),
        ],
        compiler_params=pltpu.CompilerParams(
            collective_id=0, has_side_effects=True, vmem_limit_bytes=60 * 1024 * 1024
        ),
    )(*operands)
    return solution_out, relative.reshape(()), rms.reshape(())


def solution(mesh):
    dims = (mesh.shape["wall"], mesh.shape["sx"], mesh.shape["sy"])
    return jax.shard_map(
        functools.partial(shards, dims),
        mesh=mesh,
        in_specs=(
            P("sx", "sy", "wall", None),
            P("sx", "sy", "wall", None, None),
            P("sx", "sy", "wall", None, None),
            P("sx", "sy", "wall", None, None),
            P("sx", "sy", "wall", None, None, None),
            P("sx", "sy", "wall", None),
        ),
        out_specs=(P("sx", "sy", "wall", None), P(), P()),
        check_vma=False,
    )
```

```python
import functools

import jax
import jax.numpy as jnp
import numpy as np
from jax import lax
from jax.experimental import pallas as pl
from jax.experimental.pallas import tpu as pltpu
from jax.sharding import PartitionSpec as P

PTS = 4
VARS = 6
BLOCK = 384
FACE = 96
ITERS = 3
LANES = 128
TAIL = BLOCK - FACE
MESH = pl.DeviceIdType.MESH
PAIRS = [(a, b) for a in range(ITERS + 1) for b in range(a, ITERS + 1)]


def face_nodes():
    ids = np.arange(BLOCK).reshape(PTS, PTS, PTS, VARS)
    return [ids[:, :, 0], ids[:, :, PTS - 1], ids[:, 0], ids[:, PTS - 1]]


def gather_matrices():
    faces = face_nodes()
    out = np.zeros((4, BLOCK, 4 * LANES), np.float32)
    for f, touching in enumerate((1, 0, 3, 2)):
        for turn in range(4):
            source = np.rot90(faces[touching], turn, axes=(0, 1)).reshape(-1)
            out[f, source, turn * LANES + np.arange(FACE)] = 1.0
    return out


def scatter_matrix():
    out = np.zeros((4 * FACE, BLOCK), np.float32)
    for f, nodes in enumerate(face_nodes()):
        out[f * FACE + np.arange(FACE), nodes.reshape(-1)] = 1.0
    return out


def split_rows(x):
    high = x.astype(jnp.bfloat16).astype(jnp.float32)
    rest = x - high
    middle = rest.astype(jnp.bfloat16).astype(jnp.float32)
    low = rest - middle
    pad = jnp.zeros_like(x)
    return jnp.concatenate([high, middle, low, pad], 0).astype(jnp.bfloat16)


def select_dot(x, chosen):
    rows = x.shape[0]
    y = jnp.dot(split_rows(x), chosen, preferred_element_type=jnp.float32)
    return y[:rows] + y[rows : 2 * rows] + y[2 * rows : 3 * rows]


def lane_sums(part):
    high = part.astype(jnp.bfloat16)
    low = (part - high.astype(jnp.float32)).astype(jnp.bfloat16)
    ones = jnp.ones((16, part.shape[1]), jnp.bfloat16)
    if part.shape[1] == LANES:
        high, low = jnp.concatenate([high, low], 1), None
        ones = jnp.ones((16, 2 * LANES), jnp.bfloat16)

    def total(rows):
        return lax.dot_general(ones, rows, (((1,), (1,)), ((), ())), preferred_element_type=jnp.float32)

    sums = total(high)
    return (sums if low is None else sums + total(low))[:1]


def kernel(
    dims,
    total_entries,
    f_hbm,
    piv_hbm,
    low_hbm,
    up_hbm,
    side_hbm,
    ori_hbm,
    gat_hbm,
    sca_hbm,
    sol_ref,
    rel_ref,
    rms_ref,
    f_v,
    piv,
    low,
    up,
    side,
    ori,
    gat,
    sca,
    turned,
    ubuf,
    dbuf,
    yrow,
    fwd_out,
    fwd_in,
    bwd_out,
    bwd_in,
    hx_low,
    hx_high,
    hy_low,
    hy_high,
    gram_a,
    gram_b,
    load_sem,
    piv_sem,
    wall_sem,
    halo_sem,
    a_send,
    a_recv,
    b_send,
    b_recv,
):
    W, SX, SY = dims
    X, Y, E = f_v.shape[:3]
    L = X * Y
    N = L * E
    lines = [(x, y) for x in range(X) for y in range(Y)]
    wall, sx, sy = lax.axis_index("wall"), lax.axis_index("sx"), lax.axis_index("sy")
    rank = wall * SX + sx
    n_a = W * SX

    loads = [
        pltpu.make_async_copy(src, dst, load_sem.at[i])
        for i, (src, dst) in enumerate(
            [
                (f_hbm, f_v),
                (low_hbm, low),
                (up_hbm, up),
                (gat_hbm, gat),
                (side_hbm, side),
                (ori_hbm, ori),
                (sca_hbm, sca),
            ]
        )
    ]
    piv_loads = [
        pltpu.make_async_copy(piv_hbm.at[x, y, k], piv.at[x, y, k], piv_sem.at[(x * Y + y) * E + k])
        for x, y in lines
        for k in range(E)
    ]
    loads[0].start()
    for c in piv_loads:
        c.start()
    for c in loads[1:]:
        c.start()

    for ref in (fwd_in, bwd_in, hx_low, hx_high, hy_low, hy_high, fwd_out, bwd_out):
        ref[...] = jnp.zeros(ref.shape, jnp.float32)

    barrier = pltpu.get_barrier_semaphore()

    def group_a(t):
        target = lax.rem(rank + t, n_a)
        return {"wall": target // SX, "sx": lax.rem(target, SX)}

    def group_b(t):
        return {"sy": lax.rem(sy + t, SY)}

    for t in range(1, n_a):
        pl.semaphore_signal(barrier, inc=1, device_id=group_a(t), device_id_type=MESH)
    for t in range(1, SY):
        pl.semaphore_signal(barrier, inc=1, device_id=group_b(t), device_id_type=MESH)

    loads[0].wait()
    ubuf[0] = jnp.concatenate([f_v[x, y] for x, y in lines], 0)
    lane = lax.broadcasted_iota(jnp.int32, (1, LANES), 1)

    corner_pad = jnp.zeros((LANES - FACE, LANES), jnp.float32)
    for e in range(N):
        x, y, k = e // E // Y, e // E % Y, e % E
        piv_loads[e].wait()
        turned[0, e] = jnp.concatenate([piv[x, y, k, TAIL:, :LANES], corner_pad], 0).T[:FACE]
        turned[1, e] = jnp.concatenate([piv[x, y, k, :FACE, :LANES], corner_pad], 0).T[:FACE]
        turned[2, e] = jnp.concatenate([piv[x, y, k, :FACE, TAIL - 32 :], corner_pad], 0).T[32:]
    for c in loads[1:]:
        c.wait()
    if n_a + SY > 2:
        pl.semaphore_wait(barrier, n_a + SY - 2)

    def put(columns, e, column):
        return jnp.where(lane == e, column, columns)

    row_ids = lax.broadcasted_iota(jnp.int32, (N, 1), 0)

    def put_row(rows, e, row):
        return jnp.where(row_ids == e, row, rows)

    def rows_of(columns):
        return columns.T[:N]

    def remote(src, dst, send, recv, device):
        return pltpu.make_async_remote_copy(
            src_ref=src, dst_ref=dst, send_sem=send, recv_sem=recv, device_id=device, device_id_type=MESH
        )

    def halo_copies(j):
        s = halo_sem
        return [
            (sx < SX - 1, sx > 0, remote(dbuf.at[j, X - 1], hx_low.at[j], s.at[0, 0, j], s.at[1, 0, j], {"sx": lax.rem(sx + 1, SX)})),
            (sx > 0, sx < SX - 1, remote(dbuf.at[j, 0], hx_high.at[j], s.at[0, 1, j], s.at[1, 1, j], {"sx": lax.rem(sx + SX - 1, SX)})),
            (sy < SY - 1, sy > 0, remote(dbuf.at[j, :, Y - 1], hy_low.at[j], s.at[0, 2, j], s.at[1, 2, j], {"sy": lax.rem(sy + 1, SY)})),
            (sy > 0, sy < SY - 1, remote(dbuf.at[j, :, 0], hy_high.at[j], s.at[0, 3, j], s.at[1, 3, j], {"sy": lax.rem(sy + SY - 1, SY)})),
        ]

    def wall_copies(j):
        s = wall_sem
        return (
            remote(fwd_out.at[j], fwd_in.at[j], s.at[0, 0, j], s.at[1, 0, j], {"wall": lax.rem(wall + 1, W)}),
            remote(bwd_out.at[j], bwd_in.at[j], s.at[0, 1, j], s.at[1, 1, j], {"wall": lax.rem(wall + W - 1, W)}),
        )

    def step(j, carry):
        y_all = jnp.zeros((N, BLOCK), jnp.float32)
        for e in range(N):
            x, y, k = e // E // Y, e // E % Y, e % E
            r = ubuf[j, e : e + 1, :]
            part = piv[x, y, k, :, :LANES] * r[:, :LANES]
            for c in range(1, BLOCK // LANES):
                part += piv[x, y, k, :, c * LANES : (c + 1) * LANES] * r[:, c * LANES : (c + 1) * LANES]
            y_all = put_row(y_all, e, lane_sums(part))
        yrow[...] = y_all
        ahead = y_all[:, TAIL:]

        forward, backward = wall_copies(j)

        @pl.when(wall > 0)
        def _():
            forward.wait_recv()

        u_cols = [None] * N
        s = [fwd_in[j, l : l + 1, :FACE] for l in range(L)]
        for k in range(E):
            for l, (x, y) in enumerate(lines):
                u_cols[l * E + k] = jnp.sum(low[x, y, k] * s[l], 1, keepdims=True)
            for l in range(L):
                e = l * E + k
                s[l] = ahead[e : e + 1] - jnp.sum(turned[0, e, :, :FACE] * u_cols[e], 0, keepdims=True)
        for l in range(L):
            fwd_out[j, l : l + 1, :FACE] = s[l]

        @pl.when(wall < W - 1)
        def _():
            forward.start()

        trailing = []
        u_columns = jnp.zeros((FACE, LANES), jnp.float32)
        for e in range(N):
            trailing.append(
                yrow[e : e + 1, :FACE] - jnp.sum(turned[1, e, :, :FACE] * u_cols[e], 0, keepdims=True)
            )
            u_columns = put(u_columns, e, u_cols[e])
        u_rows = rows_of(jnp.concatenate([u_columns, corner_pad], 0))

        @pl.when(wall < W - 1)
        def _():
            backward.wait_recv()

        v_columns = jnp.zeros((FACE, LANES), jnp.float32)
        t = [bwd_in[j, l : l + 1, :FACE] for l in range(L)]
        for k in reversed(range(E)):
            v = [jnp.sum(up[x, y, k] * t[l], 1, keepdims=True) for l, (x, y) in enumerate(lines)]
            for l in range(L):
                e = l * E + k
                v_columns = put(v_columns, e, v[l])
                t[l] = trailing[e] - jnp.sum(turned[2, e, :, :FACE] * v[l], 0, keepdims=True)
        for l in range(L):
            bwd_out[j, l : l + 1, :FACE] = t[l]

        @pl.when(wall > 0)
        def _():
            backward.start()

        v_rows = rows_of(jnp.concatenate([corner_pad, v_columns], 0))
        change = jnp.zeros((N, BLOCK), jnp.float32)
        for e in range(N):
            x, y, k = e // E // Y, e // E % Y, e % E
            part = piv[x, y, k, :, :LANES] * u_rows[e : e + 1]
            part += piv[x, y, k, :, BLOCK - LANES :] * v_rows[e : e + 1]
            change = put_row(change, e, lane_sums(part))
        d = yrow[...] - change
        for l, (x, y) in enumerate(lines):
            dbuf[j, x, y] = d[l * E : (l + 1) * E]

        halos = halo_copies(j)
        for sends, _, copy in halos:
            pl.when(sends)(copy.start)
        for _, receives, copy in halos:
            pl.when(receives)(copy.wait_recv)

        beside = [[], [], [], []]
        for x, y in lines:
            beside[0].append(dbuf[j, x - 1, y] if x > 0 else hx_low[j, y])
            beside[1].append(dbuf[j, x + 1, y] if x < X - 1 else hx_high[j, y])
            beside[2].append(dbuf[j, x, y - 1] if y > 0 else hy_low[j, x])
            beside[3].append(dbuf[j, x, y + 1] if y < Y - 1 else hy_high[j, x])
        turns = jnp.concatenate([ori[x, y] for x, y in lines], 0)
        picked = []
        for f in range(4):
            all_turns = select_dot(jnp.concatenate(beside[f], 0), gat[f])
            across = all_turns[:, :LANES]
            for q in range(1, 4):
                across = jnp.where(turns[:, f : f + 1] == q, all_turns[:, q * LANES : (q + 1) * LANES], across)
            picked.append(across[:, :FACE])
        coupled = jnp.zeros((N, 4 * FACE), jnp.float32)
        for e in range(N):
            x, y, k = e // E // Y, e // E % Y, e % E
            part = jnp.concatenate([side[x, y, k, f] * picked[f][e : e + 1] for f in range(4)], 0)
            coupled = put_row(coupled, e, lane_sums(part))
        ubuf[j + 1] = select_dot(coupled, sca[...])
        return carry

    lax.fori_loop(0, ITERS, step, 0)

    sums = []
    for a, b in PAIRS:
        product = ubuf[a] * ubuf[b]
        folded = product[:, :LANES]
        for c in range(1, BLOCK // LANES):
            folded += product[:, c * LANES : (c + 1) * LANES]
        sums.append(jnp.sum(folded, 0, keepdims=True))
    sums.append(jnp.zeros((16 - len(PAIRS), LANES), jnp.float32))
    gram_a[rank] = jnp.concatenate(sums, 0)
    a_copies = [
        remote(gram_a.at[rank], gram_a.at[rank], a_send.at[t - 1], a_recv.at[t - 1], group_a(t)) for t in range(1, n_a)
    ]
    for c in a_copies:
        c.start()
    for t in range(1, n_a):
        source = lax.rem(rank + n_a - t, n_a)
        remote(gram_a.at[source], gram_a.at[source], a_send.at[t - 1], a_recv.at[t - 1], group_a(t)).wait_recv()
    gram = gram_a[0]
    for i in range(1, n_a):
        gram += gram_a[i]
    gram_b[sy] = gram
    b_copies = [
        remote(gram_b.at[sy], gram_b.at[sy], b_send.at[t - 1], b_recv.at[t - 1], group_b(t)) for t in range(1, SY)
    ]
    for c in b_copies:
        c.start()
    for t in range(1, SY):
        source = lax.rem(sy + SY - t, SY)
        remote(gram_b.at[source], gram_b.at[source], b_send.at[t - 1], b_recv.at[t - 1], group_b(t)).wait_recv()
    gram = gram_b[0]
    for i in range(1, SY):
        gram += gram_b[i]
    gram = jnp.sum(gram, 1, keepdims=True)
    g = {}
    for i, (a, b) in enumerate(PAIRS):
        g[a, b] = gram[i : i + 1]

    M = ITERS
    zero = jnp.zeros((1, 1), jnp.float32)
    tri = [[zero] * (M + 1) for _ in range(M + 1)]
    for i in range(M + 1):
        rest = g[i, i]
        for p in range(i):
            rest = rest - tri[p][i] * tri[p][i]
        tri[i][i] = jnp.sqrt(jnp.maximum(rest, 0.0))
        for c in range(i + 1, M + 1):
            rest = g[i, c]
            for p in range(i):
                rest = rest - tri[p][i] * tri[p][c]
            tri[i][c] = rest / tri[i][i]
    hess = [[zero] * M for _ in range(M + 1)]
    for i in range(M + 1):
        for c in range(M):
            value = tri[i][c + 1]
            for p in range(c):
                value = value - hess[i][p] * tri[p][c]
            hess[i][c] = value / tri[c][c]
    for c in range(M):
        hess[c][c] = hess[c][c] + 1.0
    for c in range(M):
        for i in range(c + 2, M + 1):
            hess[i][c] = zero
    start = tri[0][0]
    normal = [[zero] * M for _ in range(M)]
    for a in range(M):
        for b in range(a, M):
            value = hess[0][a] * hess[0][b]
            for i in range(1, M + 1):
                value = value + hess[i][a] * hess[i][b]
            normal[a][b] = normal[b][a] = value
    right = [hess[0][a] * start for a in range(M)]
    for k in range(M):
        for i in range(k + 1, M):
            factor = normal[i][k] / normal[k][k]
            for c in range(k, M):
                normal[i][c] = normal[i][c] - factor * normal[k][c]
            right[i] = right[i] - factor * right[k]
    weights = [zero] * M
    for k in reversed(range(M)):
        value = right[k]
        for c in range(k + 1, M):
            value = value - normal[k][c] * weights[c]
        weights[k] = value / normal[k][k]
    squared = zero
    for i in range(M + 1):
        miss = start if i == 0 else zero
        for c in range(M):
            miss = miss - hess[i][c] * weights[c]
        squared = squared + miss * miss
    rel_ref[0] = (jnp.sqrt(squared) / start)[0, 0]
    rms_ref[0] = jnp.sqrt(g[0, 0] / total_entries)[0, 0]
    mixed = [zero] * M
    for k in reversed(range(M)):
        value = weights[k]
        for c in range(k + 1, M):
            value = value - tri[k][c] * mixed[c]
        mixed[k] = value / tri[k][k]
    for x, y in lines:
        out = mixed[0] * dbuf[0, x, y]
        for k in range(1, M):
            out = out + mixed[k] * dbuf[k, x, y]
        sol_ref[x, y] = out

    for c in a_copies + b_copies:
        c.wait_send()
    for j in range(ITERS):
        forward, backward = wall_copies(j)
        pl.when(wall < W - 1)(forward.wait_send)
        pl.when(wall > 0)(backward.wait_send)
        for sends, _, copy in halo_copies(j):
            pl.when(sends)(copy.wait_send)


def shards(dims, forcing, pivot_inverse, lower_face, upper_face, side_coupling, orientation):
    W, SX, SY = dims
    X, Y, E = forcing.shape[:3]
    L, N = X * Y, X * Y * E
    total_entries = forcing.size * W * SX * SY
    gather = jnp.asarray(gather_matrices(), jnp.bfloat16)
    scatter = jnp.asarray(scatter_matrix(), jnp.bfloat16)
    operands = (forcing, pivot_inverse, lower_face, upper_face, side_coupling, orientation, gather, scatter)
    f32 = jnp.float32
    dma = pltpu.SemaphoreType.DMA
    solution_out, relative, rms = pl.pallas_call(
        functools.partial(kernel, dims, total_entries),
        out_shape=(
            jax.ShapeDtypeStruct(forcing.shape, f32),
            jax.ShapeDtypeStruct((1,), f32),
            jax.ShapeDtypeStruct((1,), f32),
        ),
        in_specs=[pl.BlockSpec(memory_space=pltpu.HBM)] * len(operands),
        out_specs=(
            pl.BlockSpec(memory_space=pltpu.VMEM),
            pl.BlockSpec(memory_space=pltpu.SMEM),
            pl.BlockSpec(memory_space=pltpu.SMEM),
        ),
        scratch_shapes=[pltpu.VMEM(a.shape, a.dtype) for a in operands]
        + [
            pltpu.VMEM((3, N, FACE, LANES), f32),
            pltpu.VMEM((ITERS + 1, N, BLOCK), f32),
            pltpu.VMEM((ITERS, X, Y, E, BLOCK), f32),
            pltpu.VMEM((N, BLOCK), f32),
            pltpu.VMEM((ITERS, L, LANES), f32),
            pltpu.VMEM((ITERS, L, LANES), f32),
            pltpu.VMEM((ITERS, L, LANES), f32),
            pltpu.VMEM((ITERS, L, LANES), f32),
            pltpu.VMEM((ITERS, Y, E, BLOCK), f32),
            pltpu.VMEM((ITERS, Y, E, BLOCK), f32),
            pltpu.VMEM((ITERS, X, E, BLOCK), f32),
            pltpu.VMEM((ITERS, X, E, BLOCK), f32),
            pltpu.VMEM((W * SX, 16, LANES), f32),
            pltpu.VMEM((SY, 16, LANES), f32),
            dma((7,)),
            dma((N,)),
            dma((2, 2, ITERS)),
            dma((2, 4, ITERS)),
            dma((max(W * SX - 1, 1),)),
            dma((max(W * SX - 1, 1),)),
            dma((max(SY - 1, 1),)),
            dma((max(SY - 1, 1),)),
        ],
        compiler_params=pltpu.CompilerParams(
            collective_id=0, has_side_effects=True, vmem_limit_bytes=60 * 1024 * 1024
        ),
    )(*operands)
    return solution_out, relative.reshape(()), rms.reshape(())


def solution(mesh):
    dims = (mesh.shape["wall"], mesh.shape["sx"], mesh.shape["sy"])
    return jax.shard_map(
        functools.partial(shards, dims),
        mesh=mesh,
        in_specs=(
            P("sx", "sy", "wall", None),
            P("sx", "sy", "wall", None, None),
            P("sx", "sy", "wall", None, None),
            P("sx", "sy", "wall", None, None),
            P("sx", "sy", "wall", None, None, None),
            P("sx", "sy", "wall", None),
        ),
        out_specs=(P("sx", "sy", "wall", None), P(), P()),
        check_vma=False,
    )
```
